256 devices in a mesh: dp: 4 (over x), pipe: 4 (over y), tensor: 16 (over z, core).
Axes of the slice: x: 4, y: 4, z: 8, core: 2. Of those that a mesh axis runs over, the one named last changes fastest.
Arguments:
- embedded: bfloat16 [8, 192, 4096], P('dp', None, 'tensor'), parts along dimension 0, may hold values from -4 to 5
- lengths: int32 [8, 8], P('dp'), parts along dimension 0, may hold values from 1 to 64, 192 in all within a row
- destination: int32 [64], P('dp'), parts along dimension 0, may hold values from 0 to 15, each once
- attn_gain: bfloat16 [4, 4096], P('pipe', 'tensor'), may hold values from 0.099609375 to 1.8984375
- wq: bfloat16 [4, 4096, 4096], P('pipe', None, 'tensor'), may hold values from -2 to 2
- wk: bfloat16 [4, 4096, 1024], P('pipe', None, 'tensor'), may hold values from -1 to 1
- wv: bfloat16 [4, 4096, 1024], P('pipe', None, 'tensor'), may hold values from -1 to 1
- wo: bfloat16 [4, 4096, 4096], P('pipe', 'tensor'), may hold values from -1 to 1
- final_gain: bfloat16 [4096], P('tensor'), may hold values from 0.099609375 to 1.8984375
- score_head: bfloat16 [4096], P('tensor'), may hold values from -0.09375 to 0.09375
Outputs:
- rewards: float32 [64], P(('dp', 'tensor')), parts along dimension 0
The draws below stay inside these ranges and needn't reach their ends.
There are 4 independent parts, one for each index of `dp`. The reference program is written for one: setup_inputs(seed, part) draws one part's arguments, and reference() takes and returns one part's arrays. A program takes and returns all parts, laid end to end along the dimension named above; an argument that names none is the same for every part. Nothing has to cross between parts.
All inputs are finite; a program needn't handle non-finite values.
Results may differ from the reference program's by a relative error of at most 0.03.
Values may be sent and summed in bfloat16 or wider, within the bound.
No kernel may reach another device: no remote copies, remote signals or barrier semaphores. Data moves between devices by JAX's collectives and lax.ppermute only.
A program may use at most 64 MiB of HBM per device.

```python
import math
import jax
import jax.numpy as jnp
import numpy as np
from jax import lax

D = 4096
HEADS = 32
KVH = 8
HD = 128
MB_TOK = 192
MICRO = 2
SEGS = 8
MOST = 64
SECTIONS = 4
RESP = 16


def shared_keys(key):
    return jnp.clip(jax.random.normal(key, (SECTIONS, D, KVH * HD), jnp.float32), -4.0, 4.0) * D ** (-0.5)


def draw_wk(key, part):
    return shared_keys(key).astype(jnp.bfloat16)


def draw_wq(key, part):
    key = jax.random.fold_in(key, 7)
    noise = jnp.clip(jax.random.normal(key, (SECTIONS, D, HEADS * HD), jnp.float32), -4.0, 4.0) * D ** (-0.5)
    return noise.astype(jnp.bfloat16)


def draw_embedded(key, part):
    key = jax.random.fold_in(key, 11)
    noise_key, offset_key = jax.random.split(key)
    offset = jax.random.uniform(offset_key, (D,), jnp.float32, 0.25, 0.75)
    noise = jnp.clip(jax.random.normal(noise_key, (MICRO, MB_TOK, D), jnp.float32), -4.0, 4.0)
    return (noise + offset[None, None, :]).astype(jnp.bfloat16)


def draw_wv(key, part):
    key = jax.random.fold_in(key, 13)
    noise_key, mean_key = jax.random.split(key)
    column_mean = jax.random.uniform(mean_key, (SECTIONS, 1, KVH * HD), jnp.float32, 0.5, 1.5) * (2.5 / D)
    noise = jnp.clip(jax.random.normal(noise_key, (SECTIONS, D, KVH * HD), jnp.float32), -4.0, 4.0)
    return (noise * D ** (-0.5) + column_mean).astype(jnp.bfloat16)


def draw_wo(key, part):
    key = jax.random.fold_in(key, 17)
    noise_key, common_key = jax.random.split(key)
    width = HEADS * HD
    common = jnp.clip(jax.random.normal(common_key, (SECTIONS, 1, D), jnp.float32), -3.0, 3.0)
    strength = 0.6 * (jnp.arange(SECTIONS, dtype=jnp.float32) + 1.0) ** 1.75
    noise = jnp.clip(jax.random.normal(noise_key, (SECTIONS, width, D), jnp.float32), -4.0, 4.0)
    mixed = noise * (0.8 * width ** (-0.5)) + common * (strength[:, None, None] / width)
    return mixed.astype(jnp.bfloat16)


def level_of(own_key, shape, pieces, least, high):
    loudness, own = 1.0, jax.random.fold_in(own_key, 6)
    for axis_at, blocks in pieces:
        steps = jnp.exp(jax.random.uniform(jax.random.fold_in(own, axis_at), (blocks,), jnp.float32, least / len(pieces), high / len(pieces)))
        loudness = loudness * jnp.repeat(steps, shape[axis_at] // blocks).reshape([-1 if axis == axis_at else 1 for axis in range(len(shape))])
    return loudness


def length_profile(amount, total, reach, skew):
    loads = [(1 << 20) // math.isqrt(grade ** skew) + 1 for grade in range(2, amount + 1)]
    surplus, holding = total - reach - (amount - 1), [1] * (amount - 1)
    while surplus > 0:
        movable = [i for i in range(amount - 1) if holding[i] < reach]
        mass, remaining = sum([loads[i] for i in movable]), surplus
        for i in movable:
            more = min(reach - holding[i], max(1, remaining * loads[i] // mass), surplus)
            holding[i] = holding[i] + more
            surplus = surplus - more
    return np.array([reach] + holding)


def uneven(rng, number_of, total, most, slope):
    if number_of == 2:
        one = jax.random.randint(rng, (), max(1, total - most), min(most, total - 1) + 1)
        return jnp.stack([one, total - one])
    sizes = jnp.asarray(length_profile(number_of, total, most, slope), jnp.int32)
    couples = (number_of - 1) // 2
    donor, taker = sizes[1:1 + 2 * couples:2], sizes[2:2 + 2 * couples:2]
    slack = jnp.minimum(donor - 1, most - taker)
    moved = jax.random.randint(jax.random.fold_in(rng, 1), (couples,), 0, 1 << 20) % (slack + 1)
    sizes = sizes.at[1:1 + 2 * couples:2].set(donor - moved).at[2:2 + 2 * couples:2].set(taker + moved)
    return sizes[jax.random.permutation(jax.random.fold_in(rng, 2), number_of)]


def normal_values(stream_key, extent, scale, bound, cuts=(), held_as=jnp.bfloat16):
    factor_of = level_of(stream_key, extent, cuts, -0.22, 0.18) if cuts else 1.0
    entries = jax.random.normal(stream_key, extent, jnp.float32) * scale * factor_of
    return jnp.minimum(jnp.maximum(entries, -bound), bound).astype(held_as)


def setup_inputs(seed: int = 0, part: int = 0) -> dict:
    key_of = jax.random.split(jax.random.key(seed), 11)
    part_splits = jax.random.split(jax.random.fold_in(key_of[10], part), 11)
    return {
        "embedded": draw_embedded(jax.random.fold_in(jax.random.fold_in(key_of[10], part), 71), part),
        "lengths": jax.vmap(lambda own: uneven(own, SEGS, MB_TOK, MOST, 2))(jax.random.split(part_splits[1], MICRO)).reshape((MICRO, SEGS)).astype(jnp.int32),
        "destination": jax.random.permutation(part_splits[2], RESP).astype(jnp.int32),
        "attn_gain": jnp.clip(1.0 + 0.18 * jax.random.normal(key_of[3], (SECTIONS, D), jnp.float32), 0.099609375, 1.8984375).astype(jnp.bfloat16),
        "wq": draw_wq(jax.random.fold_in(key_of[10], 71), part),
        "wk": draw_wk(jax.random.fold_in(key_of[10], 71), part),
        "wv": draw_wv(jax.random.fold_in(key_of[10], 71), part),
        "wo": draw_wo(jax.random.fold_in(key_of[10], 71), part),
        "final_gain": jnp.clip(1.0 + 0.18 * jax.random.normal(key_of[8], (D,), jnp.float32), 0.099609375, 1.8984375).astype(jnp.bfloat16),
        "score_head": normal_values(key_of[9], (D,), D ** -0.5, 0.09375, ((0, 16),)),
    }


eps = 1e-05
rope_base = 500000.0

def segment_layout(lens):
    ends = jnp.cumsum(lens).astype(jnp.int32)
    rows = jnp.arange(MB_TOK, dtype=jnp.int32)
    passed = (rows[:, None] >= ends[None, :]).astype(jnp.int32)
    segment = lax.optimization_barrier(jnp.sum(passed, axis=1)).astype(jnp.int32)
    start = lax.optimization_barrier(jnp.sum(passed * lens[None, :], axis=1)).astype(jnp.int32)
    return (segment, rows - start, ends - 1)

def rotary(position):
    half = HD // 2
    freq = rope_base ** (-jnp.arange(half, dtype=jnp.float32) / half)
    angles = position.astype(jnp.float32)[:, None] * freq[None, :]
    return (jnp.cos(angles), jnp.sin(angles))

def rotate(values, cosine, sine):
    half = values.shape[-1] // 2
    first, second = (values[..., :half], values[..., half:])
    cos_b, sin_b = (cosine[:, None, :], sine[:, None, :])
    return jnp.concatenate([first * cos_b - second * sin_b, second * cos_b + first * sin_b], axis=-1)

def attend(state, gain, w_query, w_key, w_value, w_out, cosine, sine, allowed):
    full = state.astype(jnp.float32)
    mean_sq = lax.optimization_barrier(jnp.mean(full * full, axis=1, keepdims=True))
    normed = (full * lax.rsqrt(mean_sq + eps) * gain.astype(jnp.float32)).astype(jnp.bfloat16)
    query = jnp.dot(normed, w_query, preferred_element_type=jnp.float32).reshape(MB_TOK, HEADS, HD)
    keys = jnp.dot(normed, w_key, preferred_element_type=jnp.float32).reshape(MB_TOK, KVH, HD)
    values = jnp.dot(normed, w_value, preferred_element_type=jnp.float32).reshape(MB_TOK, KVH, HD).astype(jnp.bfloat16)
    query = rotate(query, cosine, sine).astype(jnp.bfloat16)
    keys = rotate(keys, cosine, sine).astype(jnp.bfloat16)
    group = HEADS // KVH
    grouped = query.reshape(MB_TOK, KVH, group, HD)
    scores = jnp.einsum('qkgd,skd->kgqs', grouped.astype(jnp.float32), keys.astype(jnp.float32)) * HD ** (-0.5)
    scores = jnp.where(allowed[None, None], scores, -1e+30)
    top = lax.optimization_barrier(jnp.max(scores, axis=-1, keepdims=True))
    raised = jnp.exp(scores - top)
    weights = (raised / lax.optimization_barrier(jnp.sum(raised, axis=-1, keepdims=True))).astype(jnp.bfloat16)
    attended = jnp.einsum('kgqs,skd->qkgd', weights.astype(jnp.float32), values.astype(jnp.float32))
    attended = attended.reshape(MB_TOK, HEADS * HD).astype(jnp.bfloat16)
    projected = jnp.dot(attended, w_out, preferred_element_type=jnp.float32)
    return (full + projected).astype(jnp.bfloat16)

def reference(embedded, lengths, destination, attn_gain, wq, wk, wv, wo, final_gain, score_head):
    rows = jnp.arange(MB_TOK, dtype=jnp.int32)
    results = []
    for micro in range(MICRO):
        segment, position, last = segment_layout(lengths[micro])
        cosine, sine = rotary(position)
        allowed = (segment[:, None] == segment[None, :]) & (rows[:, None] >= rows[None, :])
        state = embedded[micro]
        for layer in range(SECTIONS):
            state = attend(state, attn_gain[layer], wq[layer], wk[layer], wv[layer], wo[layer], cosine, sine, allowed)
        picked = state[last].astype(jnp.float32)
        dots = lax.optimization_barrier(jnp.sum(picked * final_gain.astype(jnp.float32) * score_head.astype(jnp.float32), axis=1))
        squares = lax.optimization_barrier(jnp.sum(picked * picked, axis=1))
        results.append(dots * lax.rsqrt(squares / D + eps))
    flat = jnp.concatenate(results)
    rewards = jnp.zeros((RESP,), jnp.float32).at[destination].set(flat)
    return rewards
```

```python
import functools

import jax
import jax.numpy as jnp
from jax import lax
from jax.experimental import pallas as pl
from jax.experimental.pallas import tpu as pltpu
from jax.sharding import PartitionSpec as P

D = 4096
HD = 128
MB_TOK = 192
MICRO = 2
SEGS = 8
AUX = 16
RESP = MICRO * SEGS

eps = 1e-05
rope_base = 500000.0
bf16 = jnp.bfloat16
f32 = jnp.float32
f16 = jnp.float16
DOWN = 2.0**-6

HALF = MB_TOK // 2
OFFSETS = (0, -1, 1, -2, 2, -3, 3, 4, 4)
PLACES = ((0, MB_TOK),) * 7 + ((0, HALF), (HALF, HALF))


def segment_layout(lens):
    ends = jnp.cumsum(lens)
    rows = jnp.arange(MB_TOK, dtype=jnp.int32)
    passed = (rows[:, None] >= ends[None, :]).astype(jnp.int32)
    segment = jnp.sum(passed, axis=1)
    start = jnp.sum(passed * lens[None, :], axis=1)
    return (segment, rows - start, ends - 1)


def rotary(position):
    half = HD // 2
    freq = rope_base ** (-jnp.arange(half, dtype=f32) / half)
    angles = position.astype(f32)[:, None] * freq[None, :]
    return (jnp.cos(angles), jnp.sin(angles))


def attention_kernel(first, final, at, *refs):
    refs = list(refs)
    pieces = [refs.pop(0) for _ in OFFSETS]
    tables = None if first else refs.pop(0)
    wq_own, wq_other, kv_own, kv_other, cosine, sine, bias = [refs.pop(0) for _ in range(7)]
    o_own, o_other = refs.pop(0), refs.pop(0)
    pick = refs.pop(0) if final else None
    if final:
        out = refs.pop(0)
    else:
        base, near_up, near_down, far_up, far_down, opposite = [refs.pop(0) for _ in range(6)]
    tables_out = refs.pop(0) if first else None
    normed, attended = refs
    width = normed.shape[2]
    chips = normed.shape[0]

    squares = []
    for piece, (_, count) in zip(pieces, PLACES):
        full = piece[pl.ds(0, count), :].astype(f32)
        squares.append(jnp.sum(full * full, axis=1, keepdims=True))
    square = sum(squares[:7]) + jnp.concatenate(squares[7:], axis=0)
    scale = lax.rsqrt(square / D + eps)
    if first:
        for number in (0, 1, 2, 3, 4, 5, 6, 8):
            count = PLACES[number][1]
            tables_out[at[number]] = pieces[number][pl.ds(count, AUX), :]
        tables = tables_out
    for number, (row, count) in enumerate(PLACES):
        shard = at[number]
        gain = tables[shard][0:1].astype(f32)
        full = pieces[number][pl.ds(0, count), :].astype(f32)
        normed[shard, pl.ds(row, count), :] = (full * scale[row : row + count] * gain).astype(bf16)
    zero = jnp.zeros((MB_TOK, wq_own.shape[1]), f32)
    query = [zero, zero]
    zero = jnp.zeros((MB_TOK, kv_own.shape[0]), f32)
    pair = [zero, zero]
    for shard in range(chips):
        part = normed[shard]
        span = pl.ds(shard * width, width)
        for side, (w, kv) in enumerate(((wq_own, kv_own), (wq_other, kv_other))):
            query[side] += jnp.dot(part, w[span, :], preferred_element_type=f32)
            pair[side] += lax.dot_general(
                part, kv[:, span], (((1,), (1,)), ((), ())), preferred_element_type=f32
            )
    lower = at[len(OFFSETS)] == 0
    front = jnp.where(lower, pair[0], pair[1])
    back = jnp.where(lower, pair[1], pair[0])
    left = lax.broadcasted_iota(jnp.int32, (MB_TOK, HD), 1) < HD // 2
    key = jnp.where(left, front, pltpu.roll(back, HD // 2, 1))
    value = jnp.where(left, pltpu.roll(front, HD // 2, 1), back).astype(bf16)
    cos_full, sin_full = cosine[...], sine[...]

    def rotated(block):
        return (block * cos_full + pltpu.roll(block, HD // 2, 1) * sin_full).astype(bf16)

    key = rotated(key)
    mask = bias[...]
    heads = wq_own.shape[1] // HD
    for head in range(2 * heads):
        within = head % heads
        rows = rotated(query[head // heads][:, within * HD : (within + 1) * HD])
        scores = lax.dot_general(
            rows, key, (((1,), (1,)), ((), ())), preferred_element_type=f32
        ) * HD ** (-0.5) + mask
        top = jnp.max(scores, axis=1, keepdims=True)
        raised = jnp.exp(scores - top)
        weights = (raised / jnp.sum(raised, axis=1, keepdims=True)).astype(bf16)
        attended[:, head * HD : (head + 1) * HD] = jnp.dot(
            weights, value, preferred_element_type=f32
        ).astype(bf16)
    half = o_own.shape[0]

    def product(rows, span):
        return jnp.dot(rows[:, :half], o_own[:, span], preferred_element_type=f32) + jnp.dot(
            rows[:, half:], o_other[:, span], preferred_element_type=f32
        )

    chip = at[len(OFFSETS) + 1]
    if not final:
        rows = attended[...]

        def term(steps):
            shard = lax.rem(chip + steps + chips, chips)
            return product(rows, pl.ds(pl.multiple_of(shard * width, width), width))

        for place, steps in enumerate((1, 3)):
            near_up[place] = term(steps)
            near_down[place] = term(-steps)
        opposite[...] = term(4)
        far_up[...] = term(2)
        far_down[...] = term(-2)
        base[...] = term(0) + pieces[0][pl.ds(0, MB_TOK), :].astype(f32)
        return
    chosen = jnp.dot(pick[...], attended[...], preferred_element_type=f32).astype(bf16)
    for shard in range(chips):
        out[shard] = product(chosen, pl.ds(shard * width, width))
    kept = jnp.dot(pick[...], pieces[0][pl.ds(0, MB_TOK), :], preferred_element_type=f32)
    out[chip] = out[chip] + kept


def call_kernel(kernel, operands, outs, scratch, flops):
    whole = pl.BlockSpec(memory_space=pltpu.VMEM)
    return pl.pallas_call(
        kernel,
        out_shape=outs,
        in_specs=[pl.BlockSpec(memory_space=pltpu.SMEM)] + [whole] * (len(operands) - 1),
        out_specs=[whole] * len(outs),
        scratch_shapes=scratch,
        compiler_params=pltpu.CompilerParams(vmem_limit_bytes=32 * 1024 * 1024),
        cost_estimate=pl.CostEstimate(
            flops=flops, bytes_accessed=8_000_000, transcendentals=150_000
        ),
    )(*operands)


def attention(first, final, at, pieces, tables, weights, angles, bias, o_rows, pick):
    width = pieces[0].shape[1]
    chips = D // width
    shape = jax.ShapeDtypeStruct
    operands = [at, *pieces] + ([] if first else [tables]) + [*weights, *angles, bias, *o_rows]
    one, two = shape((MB_TOK, width), f32), shape((2, MB_TOK, width), f32)
    outs = [one, two, two, one, one, one]
    if final:
        operands.append(pick)
        outs = [shape((chips, RESP, width), f32)]
    if first:
        outs.append(shape((chips, AUX, width), bf16))
    scratch = [pltpu.VMEM((chips, MB_TOK, width), bf16), pltpu.VMEM((MB_TOK, width), bf16)]
    kernel = functools.partial(attention_kernel, first, final)
    return call_kernel(kernel, operands, outs, scratch, 2_200_000_000)


def on_device(embedded, lengths, destination, attn_gain, wq, wk, wv, wo, final_gain, score_head):
    members = lax.axis_size("tensor")
    sections = lax.axis_size("pipe")
    chips = members // 2
    section = lax.axis_index("pipe")
    member = lax.axis_index("tensor")
    chip, core = member // 2, member % 2
    lower = core == 0
    rows = jnp.arange(MB_TOK, dtype=jnp.int32)

    def across(value):
        return lax.ppermute(value, "tensor", [(i, i ^ 1) for i in range(members)])

    def move(value, steps):
        return lax.ppermute(
            value, "tensor", [(i, (i + 2 * steps) % members) for i in range(members)]
        )

    def gather(block):
        far_up, far_down = move(block, 2), move(block, -2)
        up, down = move(block, 1), move(block, -1)
        last_up, last_down = move(far_up, 1), move(far_down, -1)
        top, bottom = move(far_up[:HALF], 2), move(far_down[HALF:], -2)
        return [block, up, down, far_up, far_down, last_up, last_down, top, bottom]

    def packed(value):
        return (value * DOWN).astype(f16)

    def unpacked(value):
        return value.astype(f32) * (1 / DOWN)

    def reduce(base, near_up, near_down, far_up, far_down, opposite):
        up, down = move(packed(near_up), 1), move(packed(near_down), -1)
        top, bottom = move(packed(opposite[:HALF]), 2), move(packed(opposite[HALF:]), -2)
        none = jnp.zeros_like(top)
        far_up = far_up + unpacked(up[1]) + unpacked(jnp.concatenate([top, none], axis=0))
        far_down = far_down + unpacked(down[1]) + unpacked(jnp.concatenate([none, bottom], axis=0))
        far_up, far_down = move(packed(far_up), 2), move(packed(far_down), -2)
        total = base + unpacked(up[0]) + unpacked(down[0])
        return (total + unpacked(far_up) + unpacked(far_down)).astype(bf16)

    mine = lax.dynamic_index_in_dim(embedded, core, 0, keepdims=False)
    theirs = lax.dynamic_index_in_dim(embedded, 1 - core, 0, keepdims=False)
    extra = jnp.concatenate(
        [
            attn_gain,
            final_gain[None, :],
            score_head[None, :],
            jnp.zeros((AUX - 3, embedded.shape[2]), bf16),
        ],
        axis=0,
    )
    mine = jnp.concatenate([mine, extra], axis=0)
    theirs = across(jnp.concatenate([theirs, extra], axis=0))
    state = jnp.where(
        lower,
        jnp.concatenate([mine, theirs], axis=1),
        jnp.concatenate([theirs, mine], axis=1),
    )
    state, wq, wk, wv, wo, lengths, destination = lax.optimization_barrier(
        (state, wq, wk, wv, wo, lengths, destination)
    )

    q_own = wq[0]
    kv_own = jnp.concatenate([wk[0].T, wv[0].T], axis=0)
    weights = (q_own, across(q_own), kv_own, across(kv_own))
    o_rows = (wo[0], across(wo[0]))

    lens = lax.dynamic_index_in_dim(lengths, core, 0, keepdims=False)
    segment, position, last = segment_layout(lens)
    cosine, sine = rotary(position)
    angles = (
        jnp.concatenate([cosine, cosine], axis=1),
        jnp.concatenate([-sine, sine], axis=1),
    )
    allowed = (segment[:, None] == segment[None, :]) & (rows[:, None] >= rows[None, :])
    bias = jnp.where(allowed, 0.0, -1e30).astype(f32)
    owners = lax.dynamic_slice_in_dim(destination, core * SEGS, SEGS)
    slots = jnp.arange(RESP, dtype=jnp.int32)
    pick = jnp.sum(
        (owners[None, :] == slots[:, None]).astype(f32)[:, :, None]
        * (last[:, None] == rows[None, :]).astype(f32)[None, :, :],
        axis=1,
    ).astype(bf16)
    at = jnp.concatenate(
        [(chip + jnp.array(OFFSETS, jnp.int32) + chips) % chips, jnp.stack([core, chip])]
    ).astype(jnp.int32)

    tables = None
    for number in range(sections):
        first, final = number == 0, number == sections - 1
        outs = attention(
            first, final, at, gather(state), tables, weights, angles, bias, o_rows, pick
        )
        if final:
            continue
        if first:
            tables = outs[6]
        state = reduce(*outs[:6])
        state = lax.ppermute(
            state, "pipe", [(i, (i + 1) % sections) for i in range(sections)]
        )
    partial = outs[0].transpose(1, 0, 2)
    ends = lax.all_to_all(partial, "tensor", 0, 0)
    ends = jnp.sum(ends, axis=0).astype(bf16).astype(f32)
    scale = tables[:, 1].astype(f32) * tables[:, 2].astype(f32)
    dot = jnp.sum(ends * scale)
    square = jnp.sum(ends * ends)
    reward = (dot * lax.rsqrt(square / D + eps)).reshape(1)
    result = reward
    for target in range(sections - 1):
        sent = lax.ppermute(reward, "pipe", [(sections - 1, target)])
        result = jnp.where(section == target, sent, result)
    return result


def solution(mesh):
    return jax.shard_map(
        on_device,
        mesh=mesh,
        in_specs=(
            P("dp", None, "tensor"),
            P("dp", None),
            P("dp"),
            P("pipe", "tensor"),
            P("pipe", None, "tensor"),
            P("pipe", None, "tensor"),
            P("pipe", None, "tensor"),
            P("pipe", "tensor", None),
            P("tensor"),
            P("tensor"),
        ),
        out_specs=P(("dp", "tensor")),
        check_vma=False,
    )
```

```python
import functools

import jax
import jax.numpy as jnp
from jax import lax
from jax.experimental import pallas as pl
from jax.experimental.pallas import tpu as pltpu
from jax.sharding import PartitionSpec as P

D = 4096
HD = 128
MB_TOK = 192
MICRO = 2
SEGS = 8
AUX = 16
RESP = MICRO * SEGS

eps = 1e-05
rope_base = 500000.0
bf16 = jnp.bfloat16
f32 = jnp.float32
f16 = jnp.float16
DOWN = 2.0**-6

HALF = MB_TOK // 2
OFFSETS = (0, -1, 1, -2, 2, -3, 3, 4, 4)
PLACES = ((0, MB_TOK),) * 7 + ((0, HALF), (HALF, HALF))


def segment_layout(lens):
    ends = jnp.cumsum(lens)
    rows = jnp.arange(MB_TOK, dtype=jnp.int32)
    passed = (rows[:, None] >= ends[None, :]).astype(jnp.int32)
    segment = jnp.sum(passed, axis=1)
    start = jnp.sum(passed * lens[None, :], axis=1)
    return (segment, rows - start, ends - 1)


def rotary(position):
    half = HD // 2
    freq = rope_base ** (-jnp.arange(half, dtype=f32) / half)
    angles = position.astype(f32)[:, None] * freq[None, :]
    return (jnp.cos(angles), jnp.sin(angles))


def attention_kernel(first, final, at, *refs):
    refs = list(refs)
    pieces = [refs.pop(0) for _ in OFFSETS]
    tables = None if first else refs.pop(0)
    wq_own, wq_other, *kv, cosine, sine, bias = [refs.pop(0) for _ in range(9)]
    o_own, o_other = refs.pop(0), refs.pop(0)
    pick = refs.pop(0) if final else None
    if final:
        out = refs.pop(0)
    else:
        base, near_up, near_down, far_up, far_down, opposite = [refs.pop(0) for _ in range(6)]
    tables_out = refs.pop(0) if first else None
    normed, attended = refs
    width = normed.shape[2]
    chips = normed.shape[0]

    squares = []
    for piece, (_, count) in zip(pieces, PLACES):
        full = piece[pl.ds(0, count), :].astype(f32)
        squares.append(jnp.sum(full * full, axis=1, keepdims=True))
    square = sum(squares[:7]) + jnp.concatenate(squares[7:], axis=0)
    scale = lax.rsqrt(square / D + eps)
    if first:
        for number in (0, 1, 2, 3, 4, 5, 6, 8):
            count = PLACES[number][1]
            tables_out[at[number]] = pieces[number][pl.ds(count, AUX), :]
        tables = tables_out
    for number, (row, count) in enumerate(PLACES):
        shard = at[number]
        gain = tables[shard][0:1].astype(f32)
        full = pieces[number][pl.ds(0, count), :].astype(f32)
        normed[shard, pl.ds(row, count), :] = (full * scale[row : row + count] * gain).astype(bf16)
    zero = jnp.zeros((MB_TOK, wq_own.shape[1]), f32)
    query = [zero, zero]
    zero = jnp.zeros((MB_TOK, HD), f32)
    pair = [zero, zero]
    for shard in range(chips):
        part = normed[shard]
        span = pl.ds(shard * width, width)
        for side, w in enumerate((wq_own, wq_other)):
            query[side] += jnp.dot(part, w[span, :], preferred_element_type=f32)
            joined = jnp.concatenate([kv[2 * side][:, span], kv[2 * side + 1][:, span]], axis=0)
            pair[side] += lax.dot_general(
                part, joined, (((1,), (1,)), ((), ())), preferred_element_type=f32
            )
    lower = at[len(OFFSETS)] == 0
    front = jnp.where(lower, pair[0], pair[1])
    back = jnp.where(lower, pair[1], pair[0])
    left = lax.broadcasted_iota(jnp.int32, (MB_TOK, HD), 1) < HD // 2
    key = jnp.where(left, front, pltpu.roll(back, HD // 2, 1))
    value = jnp.where(left, pltpu.roll(front, HD // 2, 1), back).astype(bf16)
    cos_full, sin_full = cosine[...], sine[...]

    def rotated(block):
        return (block * cos_full + pltpu.roll(block, HD // 2, 1) * sin_full).astype(bf16)

    key = rotated(key)
    mask = bias[...]
    heads = wq_own.shape[1] // HD
    for head in range(2 * heads):
        within = head % heads
        rows = rotated(query[head // heads][:, within * HD : (within + 1) * HD])
        scores = lax.dot_general(
            rows, key, (((1,), (1,)), ((), ())), preferred_element_type=f32
        ) * HD ** (-0.5) + mask
        top = jnp.max(scores, axis=1, keepdims=True)
        raised = jnp.exp(scores - top)
        weights = (raised / jnp.sum(raised, axis=1, keepdims=True)).astype(bf16)
        attended[:, head * HD : (head + 1) * HD] = jnp.dot(
            weights, value, preferred_element_type=f32
        ).astype(bf16)
    half = o_own.shape[0]

    def product(rows, span):
        return jnp.dot(rows[:, :half], o_own[:, span], preferred_element_type=f32) + jnp.dot(
            rows[:, half:], o_other[:, span], preferred_element_type=f32
        )

    chip = at[len(OFFSETS) + 1]
    if not final:
        rows = attended[...]

        def term(steps):
            shard = lax.rem(chip + steps + chips, chips)
            return product(rows, pl.ds(pl.multiple_of(shard * width, width), width))

        for place, steps in enumerate((1, 3)):
            near_up[place] = term(steps)
            near_down[place] = term(-steps)
        opposite[...] = term(4)
        far_up[...] = term(2)
        far_down[...] = term(-2)
        base[...] = term(0)
        return
    chosen = jnp.dot(pick[...], attended[...], preferred_element_type=f32).astype(bf16)
    for shard in range(chips):
        out[shard] = product(chosen, pl.ds(shard * width, width))
    kept = jnp.dot(pick[...], pieces[0][pl.ds(0, MB_TOK), :], preferred_element_type=f32)
    out[chip] = out[chip] + kept


def call_kernel(kernel, operands, outs, scratch, flops):
    whole = pl.BlockSpec(memory_space=pltpu.VMEM)
    return pl.pallas_call(
        kernel,
        out_shape=outs,
        in_specs=[pl.BlockSpec(memory_space=pltpu.SMEM)] + [whole] * (len(operands) - 1),
        out_specs=[whole] * len(outs),
        scratch_shapes=scratch,
        compiler_params=pltpu.CompilerParams(vmem_limit_bytes=20 * 1024 * 1024),
        cost_estimate=pl.CostEstimate(
            flops=flops, bytes_accessed=8_000_000, transcendentals=150_000
        ),
    )(*operands)


def attention(first, final, at, pieces, tables, weights, angles, bias, o_rows, pick):
    width = pieces[0].shape[1]
    chips = D // width
    shape = jax.ShapeDtypeStruct
    operands = [at, *pieces] + ([] if first else [tables]) + [*weights, *angles, bias, *o_rows]
    one, two = shape((MB_TOK, width), f32), shape((2, MB_TOK, width), f32)
    outs = [one, two, two, one, one, one]
    if final:
        operands.append(pick)
        outs = [shape((chips, RESP, width), f32)]
    if first:
        outs.append(shape((chips, AUX, width), bf16))
    scratch = [pltpu.VMEM((chips, MB_TOK, width), bf16), pltpu.VMEM((MB_TOK, width), bf16)]
    kernel = functools.partial(attention_kernel, first, final)
    return call_kernel(kernel, operands, outs, scratch, 2_200_000_000)


def on_device(embedded, lengths, destination, attn_gain, wq, wk, wv, wo, final_gain, score_head):
    members = lax.axis_size("tensor")
    sections = lax.axis_size("pipe")
    chips = members // 2
    section = lax.axis_index("pipe")
    member = lax.axis_index("tensor")
    chip, core = member // 2, member % 2
    lower = core == 0
    rows = jnp.arange(MB_TOK, dtype=jnp.int32)

    def across(value):
        return lax.ppermute(value, "tensor", [(i, i ^ 1) for i in range(members)])

    def move(value, steps):
        return lax.ppermute(
            value, "tensor", [(i, (i + 2 * steps) % members) for i in range(members)]
        )

    def gather(block):
        far_up, far_down = move(block, 2), move(block, -2)
        up, down = move(block, 1), move(block, -1)
        last_up, last_down = move(far_up, 1), move(far_down, -1)
        top, bottom = move(far_up[:HALF], 2), move(far_down[HALF:], -2)
        return [block, up, down, far_up, far_down, last_up, last_down, top, bottom]

    def packed(value):
        return (value * DOWN).astype(f16)

    def unpacked(value):
        return value.astype(f32) * (1 / DOWN)

    def onward(value, steps=0):
        route = [
            (at * members + i, (at + 1) % sections * members + (i + 2 * steps) % members)
            for at in range(sections)
            for i in range(members)
        ]
        return lax.ppermute(value, ("pipe", "tensor"), route)

    def reduce(kept, here, near_up, near_down, far_up, far_down, opposite):
        up, down = move(packed(near_up), 1), move(packed(near_down), -1)
        top, bottom = move(packed(opposite[:HALF]), 2), move(packed(opposite[HALF:]), -2)
        none = jnp.zeros_like(top)
        far_up = far_up + unpacked(up[1]) + unpacked(jnp.concatenate([top, none], axis=0))
        far_down = far_down + unpacked(down[1]) + unpacked(jnp.concatenate([none, bottom], axis=0))
        far_up, far_down = onward(packed(far_up), 2), onward(packed(far_down), -2)
        here = onward(packed(here + unpacked(up[0]) + unpacked(down[0])))
        total = kept.astype(f32) + unpacked(here)
        return (total + unpacked(far_up) + unpacked(far_down)).astype(bf16)

    mine = lax.dynamic_index_in_dim(embedded, core, 0, keepdims=False)
    theirs = lax.dynamic_index_in_dim(embedded, 1 - core, 0, keepdims=False)
    extra = jnp.concatenate(
        [
            attn_gain,
            final_gain[None, :],
            score_head[None, :],
            jnp.zeros((AUX - 3, embedded.shape[2]), bf16),
        ],
        axis=0,
    )
    mine = jnp.concatenate([mine, extra], axis=0)
    theirs = across(jnp.concatenate([theirs, extra], axis=0))
    state = jnp.where(
        lower,
        jnp.concatenate([mine, theirs], axis=1),
        jnp.concatenate([theirs, mine], axis=1),
    )
    own = (wq[0], wk[0].T, wv[0].T, wo[0])
    other = tuple(across(w) for w in own)
    state, other, lengths, destination = lax.optimization_barrier(
        (state, other, lengths, destination)
    )
    weights = (own[0], other[0], *own[1:3], *other[1:3])
    o_rows = (own[3], other[3])

    lens = lax.dynamic_index_in_dim(lengths, core, 0, keepdims=False)
    segment, position, last = segment_layout(lens)
    cosine, sine = rotary(position)
    angles = (
        jnp.concatenate([cosine, cosine], axis=1),
        jnp.concatenate([-sine, sine], axis=1),
    )
    allowed = (segment[:, None] == segment[None, :]) & (rows[:, None] >= rows[None, :])
    bias = jnp.where(allowed, 0.0, -1e30).astype(f32)
    owners = lax.dynamic_slice_in_dim(destination, core * SEGS, SEGS)
    slots = jnp.arange(RESP, dtype=jnp.int32)
    pick = jnp.sum(
        (owners[None, :] == slots[:, None]).astype(f32)[:, :, None]
        * (last[:, None] == rows[None, :]).astype(f32)[None, :, :],
        axis=1,
    ).astype(bf16)
    at = jnp.concatenate(
        [(chip + jnp.array(OFFSETS, jnp.int32) + chips) % chips, jnp.stack([core, chip])]
    ).astype(jnp.int32)

    tables = None
    for number in range(sections):
        first, final = number == 0, number == sections - 1
        pieces = gather(state)
        kept = onward(state[:MB_TOK])
        outs = attention(
            first, final, at, pieces, tables, weights, angles, bias, o_rows, pick
        )
        if final:
            continue
        if first:
            tables = outs[6]
        state = reduce(kept, *outs[:6])
    partial = outs[0].transpose(1, 0, 2)
    ends = lax.all_to_all(partial, "tensor", 0, 0)
    ends = jnp.sum(ends, axis=0).astype(bf16).astype(f32)
    scale = tables[:, 1].astype(f32) * tables[:, 2].astype(f32)
    dot = jnp.sum(ends * scale)
    square = jnp.sum(ends * ends)
    reward = (dot * lax.rsqrt(square / D + eps)).reshape(1)
    result = reward
    for target in range(sections - 1):
        sent = lax.ppermute(reward, "pipe", [(sections - 1, target)])
        result = jnp.where(section == target, sent, result)
    return result


def solution(mesh):
    return jax.shard_map(
        on_device,
        mesh=mesh,
        in_specs=(
            P("dp", None, "tensor"),
            P("dp", None),
            P("dp"),
            P("pipe", "tensor"),
            P("pipe", None, "tensor"),
            P("pipe", None, "tensor"),
            P("pipe", None, "tensor"),
            P("pipe", "tensor", None),
            P("tensor"),
            P("tensor"),
        ),
        out_specs=P(("dp", "tensor")),
        check_vma=False,
    )
```

```python
import functools

import jax
import jax.numpy as jnp
from jax import lax
from jax.experimental import pallas as pl
from jax.experimental.pallas import tpu as pltpu
from jax.sharding import PartitionSpec as P

D = 4096
HD = 128
MB_TOK = 192
MICRO = 2
SEGS = 8
AUX = 16
RESP = MICRO * SEGS

eps = 1e-05
rope_base = 500000.0
bf16 = jnp.bfloat16
f32 = jnp.float32
f16 = jnp.float16
DOWN = 2.0**-6

HALF = MB_TOK // 2
OFFSETS = (0, -1, 1, -2, 2, -3, 3, 4, 4)
PLACES = ((0, MB_TOK),) * 7 + ((0, HALF), (HALF, HALF))


def segment_layout(lens):
    ends = jnp.cumsum(lens)
    rows = jnp.arange(MB_TOK, dtype=jnp.int32)
    passed = (rows[:, None] >= ends[None, :]).astype(jnp.int32)
    segment = jnp.sum(passed, axis=1)
    start = jnp.sum(passed * lens[None, :], axis=1)
    return (segment, rows - start, ends - 1)


def rotary(position):
    half = HD // 2
    freq = rope_base ** (-jnp.arange(half, dtype=f32) / half)
    angles = position.astype(f32)[:, None] * freq[None, :]
    return (jnp.cos(angles), jnp.sin(angles))


def attention_kernel(first, final, at, *refs):
    refs = list(refs)
    pieces = [refs.pop(0) for _ in OFFSETS]
    tables = None if first else refs.pop(0)
    stored = [refs.pop(0) for _ in range(8)]
    cosine, sine, bias = [refs.pop(0) for _ in range(3)]
    pick = refs.pop(0) if final else None
    if final:
        out = refs.pop(0)
    else:
        base, near_up, near_down, far_up, far_down, opposite = [refs.pop(0) for _ in range(6)]
    tables_out = refs.pop(0) if first else None
    normed, attended, *held, arrived = refs
    copies = [
        pltpu.make_async_copy(stored[i], held[i], arrived.at[i]) for i in range(len(stored))
    ]
    for copy in copies:
        copy.start()
    (wq_own, k_own, v_own, wq_other, k_other, v_other, o_own, o_other) = held
    sides = ((wq_own, k_own, v_own), (wq_other, k_other, v_other))
    width = normed.shape[2]
    chips = normed.shape[0]

    squares = []
    for piece, (_, count) in zip(pieces, PLACES):
        full = piece[pl.ds(0, count), :].astype(f32)
        squares.append(jnp.sum(full * full, axis=1, keepdims=True))
    square = sum(squares[:7]) + jnp.concatenate(squares[7:], axis=0)
    scale = lax.rsqrt(square / D + eps)
    if first:
        for number in (0, 1, 2, 3, 4, 5, 6, 8):
            count = PLACES[number][1]
            tables_out[at[number]] = pieces[number][pl.ds(count, AUX), :]
        tables = tables_out
    for number, (row, count) in enumerate(PLACES):
        shard = at[number]
        gain = tables[shard][0:1].astype(f32)
        full = pieces[number][pl.ds(0, count), :].astype(f32)
        normed[shard, pl.ds(row, count), :] = (full * scale[row : row + count] * gain).astype(bf16)
    zero = jnp.zeros((MB_TOK, wq_own.shape[1]), f32)
    query = [zero, zero]
    zero = jnp.zeros((MB_TOK, HD), f32)
    pair = [zero, zero]
    for side, (w, k, v) in enumerate(sides):
        for copy in copies[3 * side : 3 * side + 3]:
            copy.wait()
        for shard in range(chips):
            part = normed[shard]
            span = pl.ds(shard * width, width)
            query[side] += jnp.dot(part, w[span, :], preferred_element_type=f32)
            joined = jnp.concatenate([k[:, span], v[:, span]], axis=0)
            pair[side] += lax.dot_general(
                part, joined, (((1,), (1,)), ((), ())), preferred_element_type=f32
            )
    lower = at[len(OFFSETS)] == 0
    front = jnp.where(lower, pair[0], pair[1])
    back = jnp.where(lower, pair[1], pair[0])
    left = lax.broadcasted_iota(jnp.int32, (MB_TOK, HD), 1) < HD // 2
    key = jnp.where(left, front, pltpu.roll(back, HD // 2, 1))
    value = jnp.where(left, pltpu.roll(front, HD // 2, 1), back).astype(bf16)
    cos_full, sin_full = cosine[...], sine[...]

    def rotated(block):
        return (block * cos_full + pltpu.roll(block, HD // 2, 1) * sin_full).astype(bf16)

    key = rotated(key)
    mask = bias[...]
    heads = wq_own.shape[1] // HD
    for head in range(2 * heads):
        within = head % heads
        rows = rotated(query[head // heads][:, within * HD : (within + 1) * HD])
        scores = lax.dot_general(
            rows, key, (((1,), (1,)), ((), ())), preferred_element_type=f32
        ) * HD ** (-0.5) + mask
        top = jnp.max(scores, axis=1, keepdims=True)
        raised = jnp.exp(scores - top)
        weights = (raised / jnp.sum(raised, axis=1, keepdims=True)).astype(bf16)
        attended[:, head * HD : (head + 1) * HD] = jnp.dot(
            weights, value, preferred_element_type=f32
        ).astype(bf16)
    for copy in copies[6:]:
        copy.wait()
    half = o_own.shape[0]

    def product(rows, span):
        return jnp.dot(rows[:, :half], o_own[:, span], preferred_element_type=f32) + jnp.dot(
            rows[:, half:], o_other[:, span], preferred_element_type=f32
        )

    chip = at[len(OFFSETS) + 1]
    if not final:
        rows = attended[...]

        def term(steps):
            shard = lax.rem(chip + steps + chips, chips)
            return product(rows, pl.ds(pl.multiple_of(shard * width, width), width))

        for place, steps in enumerate((1, 3)):
            near_up[place] = term(steps)
            near_down[place] = term(-steps)
        opposite[...] = term(4)
        far_up[...] = term(2)
        far_down[...] = term(-2)
        base[...] = term(0)
        return
    chosen = jnp.dot(pick[...], attended[...], preferred_element_type=f32).astype(bf16)
    for shard in range(chips):
        out[:, shard, :] = product(chosen, pl.ds(shard * width, width))
    kept = jnp.dot(pick[...], pieces[0][pl.ds(0, MB_TOK), :], preferred_element_type=f32)
    mine = lax.broadcasted_iota(jnp.int32, (RESP, chips, width), 1) == chip
    out[...] += jnp.where(mine, kept[:, None, :], 0.0)


def call_kernel(kernel, operands, stored, outs, scratch, flops):
    whole = pl.BlockSpec(memory_space=pltpu.VMEM)
    return pl.pallas_call(
        kernel,
        out_shape=outs,
        in_specs=[
            pl.BlockSpec(memory_space=pltpu.SMEM if i == 0 else pl.ANY if i in stored else pltpu.VMEM)
            for i in range(len(operands))
        ],
        out_specs=[whole] * len(outs),
        scratch_shapes=scratch,
        compiler_params=pltpu.CompilerParams(vmem_limit_bytes=28 * 1024 * 1024),
        cost_estimate=pl.CostEstimate(
            flops=flops, bytes_accessed=8_000_000, transcendentals=150_000
        ),
    )(*operands)


def attention(first, final, at, pieces, tables, weights, angles, bias, pick):
    width = pieces[0].shape[1]
    chips = D // width
    shape = jax.ShapeDtypeStruct
    operands = [at, *pieces] + ([] if first else [tables])
    stored = range(len(operands), len(operands) + len(weights))
    operands += [*weights, *angles, bias]
    one, two = shape((MB_TOK, width), f32), shape((2, MB_TOK, width), f32)
    outs = [one, two, two, one, one, one]
    if final:
        operands.append(pick)
        outs = [shape((RESP, chips, width), f32)]
    if first:
        outs.append(shape((chips, AUX, width), bf16))
    scratch = [pltpu.VMEM((chips, MB_TOK, width), bf16), pltpu.VMEM((MB_TOK, width), bf16)]
    scratch += [pltpu.VMEM(w.shape, bf16) for w in weights]
    scratch.append(pltpu.SemaphoreType.DMA((len(weights),)))
    kernel = functools.partial(attention_kernel, first, final)
    return call_kernel(kernel, operands, stored, outs, scratch, 2_200_000_000)


def on_device(embedded, lengths, destination, attn_gain, wq, wk, wv, wo, final_gain, score_head):
    members = lax.axis_size("tensor")
    sections = lax.axis_size("pipe")
    chips = members // 2
    section = lax.axis_index("pipe")
    member = lax.axis_index("tensor")
    chip, core = member // 2, member % 2
    lower = core == 0
    rows = jnp.arange(MB_TOK, dtype=jnp.int32)

    def across(value):
        return lax.ppermute(value, "tensor", [(i, i ^ 1) for i in range(members)])

    def move(value, steps):
        return lax.ppermute(
            value, "tensor", [(i, (i + 2 * steps) % members) for i in range(members)]
        )

    def gather(block):
        far_up, far_down = move(block, 2), move(block, -2)
        up, down = move(block, 1), move(block, -1)
        last_up, last_down = move(far_up, 1), move(far_down, -1)
        top, bottom = move(far_up[:HALF], 2), move(far_down[HALF:], -2)
        return [block, up, down, far_up, far_down, last_up, last_down, top, bottom]

    def packed(value):
        return (value * DOWN).astype(f16)

    def unpacked(value):
        return value.astype(f32) * (1 / DOWN)

    def onward(value, steps=0):
        route = [
            (at * members + i, (at + 1) % sections * members + (i + 2 * steps) % members)
            for at in range(sections)
            for i in range(members)
        ]
        return lax.ppermute(value, ("pipe", "tensor"), route)

    def reduce(kept, here, near_up, near_down, far_up, far_down, opposite):
        up, down = move(packed(near_up), 1), move(packed(near_down), -1)
        top, bottom = move(packed(opposite[:HALF]), 2), move(packed(opposite[HALF:]), -2)
        none = jnp.zeros_like(top)
        far_up = far_up + unpacked(up[1]) + unpacked(jnp.concatenate([top, none], axis=0))
        far_down = far_down + unpacked(down[1]) + unpacked(jnp.concatenate([none, bottom], axis=0))
        far_up, far_down = onward(packed(far_up), 2), onward(packed(far_down), -2)
        here = onward(packed(here + unpacked(up[0]) + unpacked(down[0])))
        total = kept.astype(f32) + unpacked(here)
        return (total + unpacked(far_up) + unpacked(far_down)).astype(bf16)

    extra = jnp.concatenate(
        [
            attn_gain,
            final_gain[None, :],
            score_head[None, :],
            jnp.zeros((AUX - 3, embedded.shape[2]), bf16),
        ],
        axis=0,
    )
    swapped, swapped_extra = across(embedded), across(extra)

    def joined(low, high, low_extra, high_extra):
        return jnp.concatenate(
            [
                jnp.concatenate([low, high], axis=1),
                jnp.concatenate([low_extra, high_extra], axis=1),
            ],
            axis=0,
        )

    state = jnp.where(
        lower,
        joined(embedded[0], swapped[0], extra, swapped_extra),
        joined(swapped[1], embedded[1], swapped_extra, extra),
    )
    own = (wq[0], wk[0].T, wv[0].T, wo[0])
    other = tuple(across(w) for w in own)
    state, other, lengths, destination = lax.optimization_barrier(
        (state, other, lengths, destination)
    )
    weights = (*own[:3], *other[:3], own[3], other[3])

    lens = lax.dynamic_index_in_dim(lengths, core, 0, keepdims=False)
    segment, position, last = segment_layout(lens)
    cosine, sine = rotary(position)
    angles = (
        jnp.concatenate([cosine, cosine], axis=1),
        jnp.concatenate([-sine, sine], axis=1),
    )
    allowed = (segment[:, None] == segment[None, :]) & (rows[:, None] >= rows[None, :])
    bias = jnp.where(allowed, 0.0, -1e30).astype(f32)
    owners = lax.dynamic_slice_in_dim(destination, core * SEGS, SEGS)
    slots = jnp.arange(RESP, dtype=jnp.int32)
    pick = jnp.sum(
        (owners[None, :] == slots[:, None]).astype(f32)[:, :, None]
        * (last[:, None] == rows[None, :]).astype(f32)[None, :, :],
        axis=1,
    ).astype(bf16)
    at = jnp.concatenate(
        [(chip + jnp.array(OFFSETS, jnp.int32) + chips) % chips, jnp.stack([core, chip])]
    ).astype(jnp.int32)

    tables = None
    for number in range(sections):
        first, final = number == 0, number == sections - 1
        pieces = gather(state)
        kept = state[:MB_TOK] if first else onward(state)
        outs = attention(
            first, final, at, pieces, tables, weights, angles, bias, pick
        )
        if final:
            continue
        if first:
            tables = outs[6]
        state = reduce(kept, *outs[:6])
    ends = lax.all_to_all(outs[0], "tensor", 0, 0)
    ends = jnp.sum(ends, axis=0).astype(bf16).astype(f32)
    scale = tables[:, 1].astype(f32) * tables[:, 2].astype(f32)
    dot = jnp.sum(ends * scale)
    square = jnp.sum(ends * ends)
    reward = (dot * lax.rsqrt(square / D + eps)).reshape(1)
    result = reward
    for target in range(sections - 1):
        sent = lax.ppermute(reward, "pipe", [(sections - 1, target)])
        result = jnp.where(section == target, sent, result)
    return result


def solution(mesh):
    return jax.shard_map(
        on_device,
        mesh=mesh,
        in_specs=(
            P("dp", None, "tensor"),
            P("dp", None),
            P("dp"),
            P("pipe", "tensor"),
            P("pipe", None, "tensor"),
            P("pipe", None, "tensor"),
            P("pipe", None, "tensor"),
            P("pipe", "tensor", None),
            P("tensor"),
            P("tensor"),
        ),
        out_specs=P(("dp", "tensor")),
        check_vma=False,
    )
```

```python
import functools

import jax
import jax.numpy as jnp
from jax import lax
from jax.experimental import pallas as pl
from jax.experimental.pallas import tpu as pltpu
from jax.sharding import PartitionSpec as P

D = 4096
HD = 128
MB_TOK = 192
MICRO = 2
SEGS = 8
AUX = 16
RESP = MICRO * SEGS

eps = 1e-05
rope_base = 500000.0
bf16 = jnp.bfloat16
f32 = jnp.float32
f16 = jnp.float16
DOWN = 2.0**-6

HALF = MB_TOK // 2
OFFSETS = (0, -1, 1, -2, 2, -3, 3, 4, 4)
PLACES = ((0, MB_TOK),) * 7 + ((0, HALF), (HALF, HALF))


def segment_layout(lens):
    ends = jnp.cumsum(lens)
    rows = jnp.arange(MB_TOK, dtype=jnp.int32)
    passed = (rows[:, None] >= ends[None, :]).astype(jnp.int32)
    segment = jnp.sum(passed, axis=1)
    start = jnp.sum(passed * lens[None, :], axis=1)
    return (segment, rows - start, ends - 1)


def rotary(position):
    half = HD // 2
    freq = rope_base ** (-jnp.arange(half, dtype=f32) / half)
    angles = position.astype(f32)[:, None] * freq[None, :]
    return (jnp.cos(angles), jnp.sin(angles))


def attention_kernel(first, final, at, *refs):
    refs = list(refs)
    pieces = [refs.pop(0) for _ in OFFSETS]
    tables = None if first else refs.pop(0)
    stored = [refs.pop(0) for _ in range(8)]
    cosine, sine, bias = [refs.pop(0) for _ in range(3)]
    pick = refs.pop(0) if final else None
    if final:
        out = refs.pop(0)
    else:
        base, near_up, near_down, far_up, far_down, opposite = [refs.pop(0) for _ in range(6)]
    tables_out = refs.pop(0) if first else None
    normed, attended, *held, arrived = refs
    copies = [
        pltpu.make_async_copy(stored[i], held[i], arrived.at[i]) for i in range(len(stored))
    ]
    for copy in copies:
        copy.start()
    (wq_own, k_own, v_own, wq_other, k_other, v_other, o_own, o_other) = held
    sides = ((wq_own, k_own, v_own), (wq_other, k_other, v_other))
    width = normed.shape[2]
    chips = normed.shape[0]

    squares = []
    for piece, (_, count) in zip(pieces, PLACES):
        full = piece[pl.ds(0, count), :].astype(f32)
        squares.append(jnp.sum(full * full, axis=1, keepdims=True))
    square = sum(squares[:7]) + jnp.concatenate(squares[7:], axis=0)
    scale = lax.rsqrt(square / D + eps)
    if first:
        for number in (0, 1, 2, 3, 4, 5, 6, 8):
            count = PLACES[number][1]
            tables_out[at[number]] = pieces[number][pl.ds(count, AUX), :]
        tables = tables_out
    for number, (row, count) in enumerate(PLACES):
        shard = at[number]
        gain = tables[shard][0:1].astype(f32)
        full = pieces[number][pl.ds(0, count), :].astype(f32)
        normed[shard, pl.ds(row, count), :] = (full * scale[row : row + count] * gain).astype(bf16)
    zero = jnp.zeros((MB_TOK, wq_own.shape[1]), f32)
    query = [zero, zero]
    zero = jnp.zeros((MB_TOK, HD), f32)
    pair = [zero, zero]
    for side, (w, k, v) in enumerate(sides):
        for copy in copies[3 * side : 3 * side + 3]:
            copy.wait()
        for shard in range(chips):
            part = normed[shard]
            span = pl.ds(shard * width, width)
            query[side] += jnp.dot(part, w[span, :], preferred_element_type=f32)
            joined = jnp.concatenate([k[:, span], v[:, span]], axis=0)
            pair[side] += lax.dot_general(
                part, joined, (((1,), (1,)), ((), ())), preferred_element_type=f32
            )
    lower = at[len(OFFSETS)] == 0
    front = jnp.where(lower, pair[0], pair[1])
    back = jnp.where(lower, pair[1], pair[0])
    left = lax.broadcasted_iota(jnp.int32, (MB_TOK, HD), 1) < HD // 2
    key = jnp.where(left, front, pltpu.roll(back, HD // 2, 1))
    value = jnp.where(left, pltpu.roll(front, HD // 2, 1), back).astype(bf16)
    cos_full, sin_full = cosine[...], sine[...]

    def rotated(block):
        return (block * cos_full + pltpu.roll(block, HD // 2, 1) * sin_full).astype(bf16)

    key = rotated(key)
    mask = bias[...]
    heads = wq_own.shape[1] // HD
    for head in range(2 * heads):
        within = head % heads
        rows = rotated(query[head // heads][:, within * HD : (within + 1) * HD])
        scores = lax.dot_general(
            rows, key, (((1,), (1,)), ((), ())), preferred_element_type=f32
        ) * HD ** (-0.5) + mask
        top = jnp.max(scores, axis=1, keepdims=True)
        raised = jnp.exp(scores - top)
        weights = (raised / jnp.sum(raised, axis=1, keepdims=True)).astype(bf16)
        attended[:, head * HD : (head + 1) * HD] = jnp.dot(
            weights, value, preferred_element_type=f32
        ).astype(bf16)
    for copy in copies[6:]:
        copy.wait()
    half = o_own.shape[0]

    def product(rows, span):
        return jnp.dot(rows[:, :half], o_own[:, span], preferred_element_type=f32) + jnp.dot(
            rows[:, half:], o_other[:, span], preferred_element_type=f32
        )

    chip = at[len(OFFSETS) + 1]
    if not final:
        rows = attended[...]

        def term(steps):
            shard = lax.rem(chip + steps + chips, chips)
            return product(rows, pl.ds(pl.multiple_of(shard * width, width), width))

        for place, steps in enumerate((1, 3)):
            near_up[place] = term(steps)
            near_down[place] = term(-steps)
        opposite[...] = term(4)
        far_up[...] = term(2)
        far_down[...] = term(-2)
        base[...] = term(0) + pieces[0][pl.ds(0, MB_TOK), :].astype(f32)
        return
    chosen = jnp.dot(pick[...], attended[...], preferred_element_type=f32).astype(bf16)
    for shard in range(chips):
        out[:, shard, :] = product(chosen, pl.ds(shard * width, width))
    kept = jnp.dot(pick[...], pieces[0][pl.ds(0, MB_TOK), :], preferred_element_type=f32)
    mine = lax.broadcasted_iota(jnp.int32, (RESP, chips, width), 1) == chip
    out[...] += jnp.where(mine, kept[:, None, :], 0.0)


def call_kernel(kernel, operands, stored, outs, scratch, flops):
    whole = pl.BlockSpec(memory_space=pltpu.VMEM)
    return pl.pallas_call(
        kernel,
        out_shape=outs,
        in_specs=[
            pl.BlockSpec(memory_space=pltpu.SMEM if i == 0 else pl.ANY if i in stored else pltpu.VMEM)
            for i in range(len(operands))
        ],
        out_specs=[whole] * len(outs),
        scratch_shapes=scratch,
        compiler_params=pltpu.CompilerParams(vmem_limit_bytes=28 * 1024 * 1024),
        cost_estimate=pl.CostEstimate(
            flops=flops, bytes_accessed=8_000_000, transcendentals=150_000
        ),
    )(*operands)


def attention(first, final, at, pieces, tables, weights, angles, bias, pick):
    width = pieces[0].shape[1]
    chips = D // width
    shape = jax.ShapeDtypeStruct
    operands = [at, *pieces] + ([] if first else [tables])
    stored = range(len(operands), len(operands) + len(weights))
    operands += [*weights, *angles, bias]
    one, two = shape((MB_TOK, width), f32), shape((2, MB_TOK, width), f32)
    outs = [one, two, two, one, one, one]
    if final:
        operands.append(pick)
        outs = [shape((RESP, chips, width), f32)]
    if first:
        outs.append(shape((chips, AUX, width), bf16))
    scratch = [pltpu.VMEM((chips, MB_TOK, width), bf16), pltpu.VMEM((MB_TOK, width), bf16)]
    scratch += [pltpu.VMEM(w.shape, bf16) for w in weights]
    scratch.append(pltpu.SemaphoreType.DMA((len(weights),)))
    kernel = functools.partial(attention_kernel, first, final)
    return call_kernel(kernel, operands, stored, outs, scratch, 2_200_000_000)


def on_device(embedded, lengths, destination, attn_gain, wq, wk, wv, wo, final_gain, score_head):
    members = lax.axis_size("tensor")
    sections = lax.axis_size("pipe")
    chips = members // 2
    section = lax.axis_index("pipe")
    member = lax.axis_index("tensor")
    chip, core = member // 2, member % 2
    lower = core == 0
    rows = jnp.arange(MB_TOK, dtype=jnp.int32)

    def across(value):
        return lax.ppermute(value, "tensor", [(i, i ^ 1) for i in range(members)])

    def move(value, steps):
        return lax.ppermute(
            value, "tensor", [(i, (i + 2 * steps) % members) for i in range(members)]
        )

    def gather(block):
        far_up, far_down = move(block, 2), move(block, -2)
        up, down = move(block, 1), move(block, -1)
        last_up, last_down = move(far_up, 1), move(far_down, -1)
        top, bottom = move(far_up[:HALF], 2), move(far_down[HALF:], -2)
        return [block, up, down, far_up, far_down, last_up, last_down, top, bottom]

    def packed(value):
        return (value * DOWN).astype(f16)

    def unpacked(value):
        return value.astype(f32) * (1 / DOWN)

    def onward(value, at):
        route = [(at * members + i, (at + 1) * members + i) for i in range(members)]
        return lax.ppermute(value, ("pipe", "tensor"), route)

    def reduce(base, near_up, near_down, far_up, far_down, opposite):
        up, down = move(packed(near_up), 1), move(packed(near_down), -1)
        top, bottom = move(packed(opposite[:HALF]), 2), move(packed(opposite[HALF:]), -2)
        none = jnp.zeros_like(top)
        far_up = far_up + unpacked(up[1]) + unpacked(jnp.concatenate([top, none], axis=0))
        far_down = far_down + unpacked(down[1]) + unpacked(jnp.concatenate([none, bottom], axis=0))
        far_up, far_down = move(packed(far_up), 2), move(packed(far_down), -2)
        total = base + unpacked(up[0]) + unpacked(down[0])
        return (total + unpacked(far_up) + unpacked(far_down)).astype(bf16)

    extra = jnp.concatenate(
        [
            attn_gain,
            final_gain[None, :],
            score_head[None, :],
            jnp.zeros((AUX - 3, embedded.shape[2]), bf16),
        ],
        axis=0,
    )
    swapped, swapped_extra = across(embedded), across(extra)

    def joined(low, high, low_extra, high_extra):
        return jnp.concatenate(
            [
                jnp.concatenate([low, high], axis=1),
                jnp.concatenate([low_extra, high_extra], axis=1),
            ],
            axis=0,
        )

    state = jnp.where(
        lower,
        joined(embedded[0], swapped[0], extra, swapped_extra),
        joined(swapped[1], embedded[1], swapped_extra, extra),
    )
    own = (wq[0], wk[0].T, wv[0].T, wo[0])
    other = tuple(across(w) for w in own)
    state, other, lengths, destination = lax.optimization_barrier(
        (state, other, lengths, destination)
    )
    weights = (*own[:3], *other[:3], own[3], other[3])

    lens = lax.dynamic_index_in_dim(lengths, core, 0, keepdims=False)
    segment, position, last = segment_layout(lens)
    cosine, sine = rotary(position)
    angles = (
        jnp.concatenate([cosine, cosine], axis=1),
        jnp.concatenate([-sine, sine], axis=1),
    )
    allowed = (segment[:, None] == segment[None, :]) & (rows[:, None] >= rows[None, :])
    bias = jnp.where(allowed, 0.0, -1e30).astype(f32)
    owners = lax.dynamic_slice_in_dim(destination, core * SEGS, SEGS)
    slots = jnp.arange(RESP, dtype=jnp.int32)
    pick = jnp.sum(
        (owners[None, :] == slots[:, None]).astype(f32)[:, :, None]
        * (last[:, None] == rows[None, :]).astype(f32)[None, :, :],
        axis=1,
    ).astype(bf16)
    at = jnp.concatenate(
        [(chip + jnp.array(OFFSETS, jnp.int32) + chips) % chips, jnp.stack([core, chip])]
    ).astype(jnp.int32)

    tables = None
    for number in range(sections):
        first, final = number == 0, number == sections - 1
        pieces = gather(state)
        outs = attention(
            first, final, at, pieces, tables, weights, angles, bias, pick
        )
        if final:
            continue
        if first:
            tables = outs[6]
        state = onward(reduce(*outs[:6]), number)
    ends = lax.all_to_all(outs[0], "tensor", 0, 0)
    ends = jnp.sum(ends, axis=0).astype(bf16).astype(f32)
    scale = tables[:, 1].astype(f32) * tables[:, 2].astype(f32)
    dot = jnp.sum(ends * scale)
    square = jnp.sum(ends * ends)
    reward = (dot * lax.rsqrt(square / D + eps)).reshape(1)
    result = reward
    for target in range(sections - 1):
        sent = lax.ppermute(reward, "pipe", [(sections - 1, target)])
        result = jnp.where(section == target, sent, result)
    return result


def solution(mesh):
    return jax.shard_map(
        on_device,
        mesh=mesh,
        in_specs=(
            P("dp", None, "tensor"),
            P("dp", None),
            P("dp"),
            P("pipe", "tensor"),
            P("pipe", None, "tensor"),
            P("pipe", None, "tensor"),
            P("pipe", None, "tensor"),
            P("pipe", "tensor", None),
            P("tensor"),
            P("tensor"),
        ),
        out_specs=P(("dp", "tensor")),
        check_vma=False,
    )
```
